32 devices in a mesh: sub: 8 (over z, y), case: 4 (over x, core).
Axes of the slice: x: 2, y: 2, z: 4, core: 2. Of those that a mesh axis runs over, the one named last changes fastest.
Arguments:
- multipliers: float32 [64, 12288], P('case', 'sub'), may hold values from -6 to 6
- right_side: float32 [64, 12288], P('case', 'sub')
- dual_ops: bfloat16 [12288, 1536], P('sub'), as said below
- glue_match: int32 [8, 2, 128], P('sub'), may hold values from 0 to 127, as said below
- mortar: bfloat16 [8, 4, 128, 128], P('sub'), may hold values from -0.5 to 0.5
- contact_ids: int32 [8, 4], P('sub'), may hold values from 0 to 3
- contact_count: int32 [8], P('sub'), may hold values from 1 to 4
Outputs:
- solved: float32 [64, 12288], P('case', 'sub')
- grad_norm: float32 [1], replicated
The draws below stay inside these ranges and needn't reach their ends.
Inputs may be any that keep to these rules, and one draw needn't show every extreme that they name: glue_match[s,1] is a permutation of 0 to 127, and glue_match[(s+1) mod 8,0] is its inverse. `dual_ops`: each subdomain's block is symmetric positive definite.
All inputs are finite; a program needn't handle non-finite values.
Results may differ from the reference program's by a relative error of at most 0.002.
Values may be sent and summed in bfloat16 or wider, within the bound.
A program may use at most 64 MiB of HBM per device.

```python
import jax
import jax.numpy as jnp
from jax import lax

M = 1536
BLK = 128
C = 64
ITERS = 4
SUBS = 8
N_SUB = 8


def draw_dual_ops(key, part):
    key_noise = jax.random.fold_in(key, 11)
    key_diag = jax.random.fold_in(key, 12)
    noise = jax.random.normal(key_noise, (SUBS, M, M), jnp.float32)
    symmetric = (noise + jnp.swapaxes(noise, 1, 2)) * (0.35 / jnp.sqrt(2.0 * M))
    diagonal = jax.random.uniform(key_diag, (SUBS, M), jnp.float32, 1.0, 2.0)
    operators = symmetric + diagonal[:, :, None] * jnp.eye(M, dtype=jnp.float32)[None]
    return operators.reshape(SUBS * M, M).astype(jnp.bfloat16)


def draw_right_side(key, part):
    key_base = jax.random.fold_in(key, 31)
    key_rough = jax.random.fold_in(key, 32)
    base = jax.random.normal(key_base, (C, SUBS, M), jnp.float32)
    sub_rise = 4.0 ** (jnp.arange(SUBS, dtype=jnp.float32) / (SUBS - 1))
    case_rise = 3.0 ** (jnp.arange(C, dtype=jnp.float32) / (C - 1))
    rough = jax.random.uniform(key_rough, (SUBS, M), jnp.float32, 0.5, 1.5)
    values = base * sub_rise[None, :, None] * rough[None] * case_rise[:, None, None]
    return values.reshape(C, SUBS * M)


def draw_glue_match(key, part):
    keys = jax.random.split(jax.random.fold_in(key, 21), SUBS)
    perms = jax.vmap(lambda single: jax.random.permutation(single, BLK))(keys).astype(jnp.int32)
    inverse = jnp.argsort(perms, axis=1).astype(jnp.int32)
    first = jnp.roll(inverse, 1, axis=0)
    return jnp.stack([first, perms], axis=1)


def draw_contact_count(key, part):
    key_counts = jax.random.fold_in(key, 41)
    key_full = jax.random.fold_in(key, 42)
    key_low = jax.random.fold_in(key, 43)
    counts = jax.random.randint(key_counts, (SUBS,), 1, 5)
    full_at = jax.random.randint(key_full, (), 0, SUBS)
    low_at = (full_at + 1 + jax.random.randint(key_low, (), 0, SUBS - 1)) % SUBS
    counts = counts.at[full_at].set(4).at[low_at].set(1)
    return counts.astype(jnp.int32)


def set_ends(result, stream_key, smallest, top_value):
    place = [jax.random.randint(jax.random.fold_in(stream_key, axis), (), 0, length) for axis, length in enumerate(result.shape)]
    longest = result.shape.index(max(result.shape))
    beside = place[:longest] + [(place[longest] + 1) % result.shape[longest]] + place[longest + 1:]
    return result.at[tuple(place)].set(smallest).at[tuple(beside)].set(top_value)


def level_of(rng, shape, cuts, low, high):
    def one(position, blocks):
        steps = jax.random.uniform(jax.random.fold_in(jax.random.fold_in(rng, 6), position), (blocks,), jnp.float32, low / len(cuts), high / len(cuts))
        return jnp.repeat(jnp.exp(steps), shape[position] // blocks).reshape((-1,) + (1,) * (len(shape) - position - 1))

    gain = one(*cuts[0])
    for cut in cuts[1:]:
        gain = gain * one(*cut)
    return gain


def centred(stream_key, shape, deviation, reach, cuts=(), kind=jnp.bfloat16):
    values = deviation * jax.random.normal(stream_key, shape, jnp.float32)
    if cuts:
        values = values * level_of(stream_key, shape, cuts, -0.22, 0.18)
    return jnp.clip(values, -reach, reach).astype(kind)


def setup_inputs(seed: int = 0) -> dict:
    arg_keys = jax.random.split(jax.random.key(seed), 8)
    return {
        "multipliers": centred(arg_keys[0], (C, SUBS * M), 1.0, 6.0, ((0, 4), (1, 8)), jnp.float32),
        "right_side": draw_right_side(jax.random.fold_in(arg_keys[7], 71), 0),
        "dual_ops": draw_dual_ops(jax.random.fold_in(arg_keys[7], 71), 0),
        "glue_match": draw_glue_match(jax.random.fold_in(arg_keys[7], 71), 0),
        "mortar": centred(arg_keys[4], (SUBS, 4, BLK, BLK), BLK ** -0.5, 0.5, ((0, 8),)),
        "contact_ids": set_ends(jax.random.randint(arg_keys[5], (SUBS, 4), 0, 4), jax.random.fold_in(arg_keys[5], 1), 0, 3).astype(jnp.int32),
        "contact_count": draw_contact_count(jax.random.fold_in(arg_keys[7], 71), 0),
    }


penalty = 0.5
exact_mode = lax.Precision.HIGHEST

def apply_operator(vector, dual_ops, glue_match, mortar, contact_ids, contact_count):
    case_cols = vector.shape[0]
    pieces = jnp.swapaxes(vector.astype(jnp.bfloat16).reshape(case_cols, N_SUB, M), 0, 1)
    operators = dual_ops.reshape(N_SUB, M, M)

    def one_product(pair):
        return jnp.dot(pair[0], pair[1], preferred_element_type=jnp.float32)
    local_part = jnp.swapaxes(lax.map(one_product, (pieces, operators)), 0, 1)
    mortar_f = mortar.astype(jnp.float32)
    blocks = vector.reshape(case_cols, N_SUB, 12, BLK)
    prev_face = jnp.roll(blocks[:, :, 1, :], 1, axis=1)
    next_face = jnp.roll(blocks[:, :, 0, :], -1, axis=1)
    first_index = jnp.broadcast_to(glue_match[None, :, 0, :], (case_cols, N_SUB, BLK))
    second_index = jnp.broadcast_to(glue_match[None, :, 1, :], (case_cols, N_SUB, BLK))
    swapped_first = jnp.take_along_axis(prev_face, first_index, axis=2)
    swapped_second = jnp.take_along_axis(next_face, second_index, axis=2)
    face_part = penalty * (blocks[:, :, 0:2, :] - jnp.stack([swapped_first, swapped_second], axis=2))
    own_blocks = blocks[:, :, 2:6, :]
    slave_blocks = jnp.roll(own_blocks, N_SUB // 2, axis=1)
    onehot = (contact_ids[:, :, None] == jnp.arange(4, dtype=jnp.int32)[None, None, :]).astype(jnp.float32)
    selected = jnp.einsum('nkb,cnbe->cnke', onehot, slave_blocks, precision=exact_mode)
    active = (jnp.arange(4, dtype=jnp.int32)[None, :] < contact_count[:, None]).astype(jnp.float32)
    mortar_jump = (jnp.einsum('cnke,nkef->cnkf', selected, mortar_f, precision=exact_mode) - own_blocks) * active[None, :, :, None]
    reply_rows = jnp.einsum('cnkf,nkef->cnke', mortar_jump, mortar_f, precision=exact_mode)
    back_rows = jnp.einsum('nkb,cnke->cnbe', onehot, reply_rows, precision=exact_mode)
    returned = jnp.roll(back_rows, N_SUB // 2, axis=1)
    correction = jnp.concatenate([face_part, returned - mortar_jump, jnp.zeros((case_cols, N_SUB, 6, BLK), jnp.float32)], axis=2)
    return local_part.reshape(case_cols, N_SUB * M) + correction.reshape(case_cols, N_SUB * M)

def reference(multipliers, right_side, dual_ops, glue_match, mortar, contact_ids, contact_count):
    current = multipliers
    grad_norms = jnp.zeros((multipliers.shape[0],), jnp.float32)
    for iteration in range(ITERS):
        gradient = apply_operator(current, dual_ops, glue_match, mortar, contact_ids, contact_count) - right_side
        grad_norms = lax.optimization_barrier(jnp.sum(gradient * gradient, axis=1))
        curved = apply_operator(gradient, dual_ops, glue_match, mortar, contact_ids, contact_count)
        grad_curves = lax.optimization_barrier(jnp.sum(gradient * curved, axis=1))
        step_size = grad_norms / grad_curves
        moved = current - step_size[:, None] * gradient
        moved_blocks = moved.reshape(moved.shape[0], N_SUB, 12, BLK)
        clipped = jnp.concatenate([moved_blocks[:, :, 0:2], jnp.maximum(moved_blocks[:, :, 2:6], 0.0), moved_blocks[:, :, 6:12]], axis=2)
        current = clipped.reshape(moved.shape)
    return (current, jnp.sqrt(jnp.sum(grad_norms)).reshape(1))
```

```python
import functools

import jax
import jax.numpy as jnp
from jax import lax
from jax.experimental import pallas as pl
from jax.experimental.pallas import tpu as pltpu
from jax.sharding import PartitionSpec as P

ITERS = 4
BLK = 128
SLOTS = 4
PENALTY = 0.5
MESH = pl.DeviceIdType.MESH
F32 = jnp.float32
BF16 = jnp.bfloat16


def radices(count):
    out = []
    while count > 1:
        factor = next(f for f in (8, 7, 6, 5, 4, 3, 2, count) if count % f == 0)
        out.append(factor)
        count //= factor
    return out


def halves(value):
    high = value.astype(BF16)
    low = (value - high.astype(F32)).astype(BF16)
    return jnp.concatenate([high, low], axis=0)


def times(value, weight, transposed=False):
    rows = value.shape[0]
    dims = (((1,), (1 if transposed else 0,)), ((), ()))
    both = lax.dot_general(halves(value), weight, dims, preferred_element_type=F32)
    return both[:rows] + both[rows:]


def kernel(
    n, nc, factors, chunks,
    x0_ref, b_ref, k_hbm, match_ref, mortar_ref, ids_ref, count_ref,
    out_ref, norm_ref,
    k_ref, x_ref, g_ref, kx_ref, q_ref, sx_ref, xp_ref, perm_ref, pack_ref, pack_p, mort_p,
    con_send, con_recv, prev_recv, next_recv, sum_send, sum_recv, tot_ref, tot_recv,
    k_sem, ex_send, ex_recv, st_send, st_recv, rel_send, rel_recv, sum_ssem, sum_rsem, tot_ssem, tot_rsem,
):
    rows = x0_ref.shape[0]
    me, cs = lax.axis_index("sub"), lax.axis_index("case")
    nxt, prv, part = lax.rem(me + 1, n), lax.rem(me + n - 1, n), lax.rem(me + n // 2, n)
    depth = k_ref.shape[0] // chunks
    per = SLOTS // nc if SLOTS % nc == 0 else SLOTS
    relayed = per < SLOTS
    contact = pl.ds(2 * BLK, SLOTS * BLK)

    k_copies = [
        pltpu.make_async_copy(
            k_hbm.at[pl.ds(i * depth, depth)], k_ref.at[pl.ds(i * depth, depth)], k_sem.at[i]
        )
        for i in range(chunks)
    ]
    for copy in k_copies:
        copy.start()

    barrier = pltpu.get_barrier_semaphore()
    greeted = 0

    def greet(sub, case):
        pl.semaphore_signal(barrier, inc=1, device_id=(sub, case), device_id_type=MESH)

    stride = 1
    rounds = []
    for f in factors:
        digit = lax.rem(me // stride, f)
        base = me - digit * stride
        rounds.append((f, stride, digit, base))
        for j in range(1, f):
            greet(base + lax.rem(digit + j, f) * stride, cs)
            greeted += 1
        stride *= f
    if len(factors) > 1:
        for other in (nxt, prv, part):
            greet(other, cs)
            greeted += 1
    for j in range(1, nc):
        greet(me, lax.rem(cs + j, nc))
        greeted += 1

    con_send[0] = x0_ref[:, 2 * BLK:(2 + SLOTS) * BLK].astype(BF16)
    line = lax.broadcasted_iota(jnp.int32, (1, BLK), 1) * 0
    for k in range(SLOTS):
        for b in range(SLOTS):
            pack_ref[k * SLOTS + b:k * SLOTS + b + 1, :] = jnp.where(line + ids_ref[0, k] == b, 1.0, 0.0)
        live = SLOTS * SLOTS + k
        pack_ref[live:live + 1, :] = jnp.where(line + count_ref[0] > k, 1.0, 0.0)
    pack_ref[SLOTS * SLOTS + SLOTS:, :] = jnp.zeros((SLOTS, BLK), F32)
    lanes = lax.broadcasted_iota(jnp.int32, (BLK, BLK), 0)
    for side in range(2):
        perm_ref[side] = jnp.where(lanes == match_ref[0, side:side + 1, :], 1.0, 0.0).astype(BF16)

    pl.semaphore_wait(barrier, greeted)

    def remote(src, dst, ssem, rsem, sub, case):
        return pltpu.make_async_remote_copy(
            src_ref=src, dst_ref=dst, send_sem=ssem, recv_sem=rsem,
            device_id=(sub, case), device_id_type=MESH,
        )

    def exchange(vec_ref, slot):
        return [
            remote(con_send.at[slot], con_recv.at[slot], ex_send.at[slot, 0], ex_recv.at[slot, 0], part, cs),
            remote(vec_ref.at[:, pl.ds(BLK, BLK)], prev_recv.at[slot], ex_send.at[slot, 1], ex_recv.at[slot, 1], nxt, cs),
            remote(vec_ref.at[:, pl.ds(0, BLK)], next_recv.at[slot], ex_send.at[slot, 2], ex_recv.at[slot, 2], prv, cs),
        ]

    first = exchange(x0_ref, 0)
    mine = pl.ds(cs * per, per) if relayed else pl.ds(0, SLOTS)
    static = [
        remote(pack_ref, pack_p, st_send.at[0], st_recv.at[0], part, cs),
        remote(mortar_ref.at[0, mine], mort_p.at[mine], st_send.at[1], st_recv.at[1], part, cs),
    ]
    for copy in first + static:
        copy.start()

    x_ref[...] = x0_ref[...]
    for i in range(chunks):
        k_copies[i].wait()
        term = jnp.dot(
            x0_ref[:, i * depth:(i + 1) * depth].astype(BF16), k_ref[i * depth:(i + 1) * depth, :],
            preferred_element_type=F32,
        )
        if i == 0:
            kx_ref[...] = term
        else:
            kx_ref[...] += term

    static[1].wait_recv()
    if relayed:
        relays = []
        for j in range(1, nc):
            copy = remote(mort_p.at[mine], mort_p.at[mine], rel_send.at[j - 1], rel_recv.at[j - 1], me, lax.rem(cs + j, nc))
            copy.start()
            relays.append(copy)

    for copy in first:
        copy.wait()
    static[0].wait()
    sx_ref[0] = times(prev_recv[0], perm_ref[0])
    sx_ref[1] = times(next_recv[0], perm_ref[1])
    xp_ref[...] = con_recv[0].astype(F32)
    static[1].wait_send()
    if relayed:
        for j in range(1, nc):
            from_other = pl.ds(lax.rem(cs + nc - j, nc) * per, per)
            remote(
                mort_p.at[from_other], mort_p.at[from_other], rel_send.at[j - 1], rel_recv.at[j - 1],
                me, lax.rem(cs + j, nc),
            ).wait_recv()
        for copy in relays:
            copy.wait_send()

    row = lax.broadcasted_iota(jnp.int32, (rows, BLK), 0)
    lane = lax.broadcasted_iota(jnp.int32, (rows, BLK), 1)

    def block(value, b):
        return value[:, b * BLK:(b + 1) * BLK]

    def chosen(pack, value, k):
        total = pack[k * SLOTS:k * SLOTS + 1, :] * block(value, 0)
        for b in range(1, SLOTS):
            total += pack[k * SLOTS + b:k * SLOTS + b + 1, :] * block(value, b)
        return total

    def live(pack, k):
        return pack[SLOTS * SLOTS + k:SLOTS * SLOTS + k + 1, :]

    def body(it, carry):
        slot = it + 1
        own, other = pack_ref[...], pack_p[...]
        x, xp = x_ref[:, 2 * BLK:(2 + SLOTS) * BLK], xp_ref[...]
        replies = [jnp.zeros((rows, BLK), F32)] * SLOTS
        for k in range(SLOTS):
            jump_p = (times(chosen(other, x, k), mort_p[k]) - block(xp, k)) * live(other, k)
            back = times(jump_p, mort_p[k], True)
            for b in range(SLOTS):
                replies[b] = replies[b] + other[k * SLOTS + b:k * SLOTS + b + 1, :] * back
        for k in range(SLOTS):
            at = slice((2 + k) * BLK, (3 + k) * BLK)
            jump = (times(chosen(own, xp, k), mortar_ref[0, k]) - block(x, k)) * live(own, k)
            grad = kx_ref[:, at] + (replies[k] - jump) - b_ref[:, at]
            g_ref[:, at] = grad
            con_send[slot, :, k * BLK:(k + 1) * BLK] = grad.astype(BF16)
        for side in range(2):
            at = slice(side * BLK, (side + 1) * BLK)
            g_ref[:, at] = kx_ref[:, at] + PENALTY * (x_ref[:, at] - sx_ref[side]) - b_ref[:, at]
        moved = exchange(g_ref, slot)
        for copy in moved:
            copy.start()
        rest = slice((2 + SLOTS) * BLK, None)
        g_ref[:, rest] = kx_ref[:, rest] - b_ref[:, rest]

        g = g_ref[...]
        q_ref[...] = jnp.dot(g.astype(BF16), k_ref[...], preferred_element_type=F32)
        q = q_ref[...]
        norm = curve = jnp.zeros((rows, BLK), F32)
        for b in range(g.shape[1] // BLK):
            norm += block(g, b) * block(g, b)
            curve += block(g, b) * block(q, b)
        for copy in moved:
            copy.wait()
        sg = [times(prev_recv[slot], perm_ref[0]), times(next_recv[slot], perm_ref[1])]
        for side in range(2):
            curve += PENALTY * block(g, side) * (block(g, side) - sg[side])
        gp = con_recv[slot].astype(F32)
        for k in range(SLOTS):
            image = jnp.dot(chosen(own, gp, k).astype(BF16), mortar_ref[0, k], preferred_element_type=F32)
            jump = (image - block(g, 2 + k)) * live(own, k)
            curve += jump * jump
        norm = jnp.sum(norm, axis=1, keepdims=True)
        curve = jnp.sum(curve, axis=1, keepdims=True)
        packed = jnp.where(lane == row, norm, 0.0) + jnp.where(lane == row + rows, curve, 0.0)
        total = jnp.sum(packed, axis=0, keepdims=True)
        for r, (f, stride, digit, base) in enumerate(rounds):
            sum_send[it, r] = total
            sum_recv[it, r, digit] = total
            sends = []
            for j in range(1, f):
                copy = remote(
                    sum_send.at[it, r], sum_recv.at[it, r, digit], sum_ssem.at[it, r, j], sum_rsem.at[it, r, digit],
                    base + lax.rem(digit + j, f) * stride, cs,
                )
                copy.start()
                sends.append(copy)
            for j in range(1, f):
                source = lax.rem(digit + j, f)
                remote(
                    sum_send.at[it, r], sum_recv.at[it, r, source], sum_ssem.at[it, r, j], sum_rsem.at[it, r, source],
                    base + source * stride, cs,
                ).wait_recv()
            total = sum_recv[it, r, 0]
            for d in range(1, f):
                total = total + sum_recv[it, r, d]
            for copy in sends:
                copy.wait_send()
        tot_ref[...] = total
        wide = jnp.broadcast_to(total, (rows, BLK))
        top = jnp.sum(jnp.where(lane == row, wide, 0.0), axis=1, keepdims=True)
        bottom = jnp.sum(jnp.where(lane == row + rows, wide, 0.0), axis=1, keepdims=True)
        step = top / bottom
        step_wide = jnp.broadcast_to(step, (rows, BLK))

        clipped = []
        for b in range(g.shape[1] // BLK):
            at = slice(b * BLK, (b + 1) * BLK)
            fresh = x_ref[:, at] - step_wide * block(g, b)
            if 2 <= b < 2 + SLOTS:
                kept = jnp.maximum(fresh, 0.0)
                clipped.append((kept - fresh).astype(BF16))
                fresh = kept
            x_ref[:, at] = fresh
        for k in range(SLOTS):
            at = slice(k * BLK, (k + 1) * BLK)
            xp_ref[:, at] = jnp.maximum(xp_ref[:, at] - step_wide * block(gp, k), 0.0)
        for side in range(2):
            sx_ref[side] = sx_ref[side] - step_wide * sg[side]

        @pl.when(it < ITERS - 1)
        def _():
            pushed = jnp.dot(
                jnp.concatenate(clipped, axis=1), k_ref[2 * BLK:(2 + SLOTS) * BLK, :], preferred_element_type=F32
            )
            for b in range(g.shape[1] // BLK):
                at = slice(b * BLK, (b + 1) * BLK)
                kx_ref[:, at] = kx_ref[:, at] - step_wide * q_ref[:, at] + block(pushed, b)

        return carry

    lax.fori_loop(0, ITERS, body, 0)

    tot_recv[cs] = tot_ref[...]
    sends = []
    for j in range(1, nc):
        copy = remote(tot_ref, tot_recv.at[cs], tot_ssem.at[j], tot_rsem.at[cs], me, lax.rem(cs + j, nc))
        copy.start()
        sends.append(copy)
    out_ref[...] = x_ref[...]
    for j in range(1, nc):
        source = lax.rem(cs + j, nc)
        remote(tot_ref, tot_recv.at[source], tot_ssem.at[j], tot_rsem.at[source], me, source).wait_recv()
    for copy in sends:
        copy.wait_send()
    total = tot_recv[0]
    for d in range(1, nc):
        total = total + tot_recv[d]
    flat = lax.broadcasted_iota(jnp.int32, (1, BLK), 1)
    whole = jnp.sum(jnp.where(flat < rows, total, 0.0), axis=1, keepdims=True)
    norm_ref[0] = jnp.sqrt(whole)[0, 0]


def solution(mesh):
    n, nc = mesh.shape["sub"], mesh.shape["case"]
    factors = radices(n)
    chunks = 3

    def on_device(multipliers, right_side, dual_ops, glue_match, mortar, contact_ids, contact_count):
        rows, order = multipliers.shape
        top = max(factors)
        rounds = len(factors)
        vmem = pl.BlockSpec(memory_space=pltpu.VMEM)
        smem = pl.BlockSpec(memory_space=pltpu.SMEM)
        dma = pltpu.SemaphoreType.DMA
        slots = ITERS + 1
        return pl.pallas_call(
            functools.partial(kernel, n, nc, factors, chunks),
            out_shape=(
                jax.ShapeDtypeStruct((rows, order), F32),
                jax.ShapeDtypeStruct((1,), F32),
            ),
            in_specs=[vmem, vmem, pl.BlockSpec(memory_space=pl.ANY), vmem, vmem, smem, smem],
            out_specs=(vmem, smem),
            scratch_shapes=[
                pltpu.VMEM((order, order), BF16),
                pltpu.VMEM((rows, order), F32),
                pltpu.VMEM((rows, order), F32),
                pltpu.VMEM((rows, order), F32),
                pltpu.VMEM((rows, order), F32),
                pltpu.VMEM((2, rows, BLK), F32),
                pltpu.VMEM((rows, SLOTS * BLK), F32),
                pltpu.VMEM((2, BLK, BLK), BF16),
                pltpu.VMEM((SLOTS * SLOTS + 2 * SLOTS, BLK), F32),
                pltpu.VMEM((SLOTS * SLOTS + 2 * SLOTS, BLK), F32),
                pltpu.VMEM((SLOTS, BLK, BLK), BF16),
                pltpu.VMEM((slots, rows, SLOTS * BLK), BF16),
                pltpu.VMEM((slots, rows, SLOTS * BLK), BF16),
                pltpu.VMEM((slots, rows, BLK), F32),
                pltpu.VMEM((slots, rows, BLK), F32),
                pltpu.VMEM((ITERS, rounds, 1, BLK), F32),
                pltpu.VMEM((ITERS, rounds, top, 1, BLK), F32),
                pltpu.VMEM((1, BLK), F32),
                pltpu.VMEM((nc, 1, BLK), F32),
                dma((chunks,)),
                dma((slots, 3)),
                dma((slots, 3)),
                dma((2,)),
                dma((2,)),
                dma((max(nc - 1, 1),)),
                dma((max(nc - 1, 1),)),
                dma((ITERS, rounds, top)),
                dma((ITERS, rounds, top)),
                dma((nc,)),
                dma((nc,)),
            ],
            compiler_params=pltpu.CompilerParams(
                collective_id=0, has_side_effects=True, vmem_limit_bytes=24 * 1024 * 1024
            ),
        )(multipliers, right_side, dual_ops, glue_match, mortar, contact_ids, contact_count)

    in_specs = (
        P("case", "sub"),
        P("case", "sub"),
        P("sub", None),
        P("sub", None, None),
        P("sub", None, None, None),
        P("sub", None),
        P("sub"),
    )
    return jax.shard_map(
        on_device, mesh=mesh, in_specs=in_specs, out_specs=(P("case", "sub"), P()), check_vma=False
    )
```

```python
import functools

import jax
import jax.numpy as jnp
from jax import lax
from jax.experimental import pallas as pl
from jax.experimental.pallas import tpu as pltpu
from jax.sharding import PartitionSpec as P

ITERS = 4
BLK = 128
SLOTS = 4
PENALTY = 0.5
MESH = pl.DeviceIdType.MESH
F32 = jnp.float32
BF16 = jnp.bfloat16


def radices(count):
    out = []
    while count > 1:
        factor = next(f for f in (8, 7, 6, 5, 4, 3, 2, count) if count % f == 0)
        out.append(factor)
        count //= factor
    return out


def halves(value):
    high = value.astype(BF16)
    low = (value - high.astype(F32)).astype(BF16)
    return jnp.concatenate([high, low], axis=0)


def times(value, weight, transposed=False):
    rows = value.shape[0]
    dims = (((1,), (1 if transposed else 0,)), ((), ()))
    both = lax.dot_general(halves(value), weight, dims, preferred_element_type=F32)
    return both[:rows] + both[rows:]


def kernel(
    n, nc, factors, chunks,
    x0_hbm, b_hbm, k_hbm, match_hbm, mortar_hbm, ids_hbm, count_hbm,
    out_ref, norm_ref,
    x0_ref, b_ref, match_ref, mortar_ref, ids_ref, count_ref,
    k_ref, x_ref, g_ref, kx_ref, q_ref, sx_ref, xp_ref, perm_ref, pack_ref, pack_p, mort_p,
    con_send, con_recv, prev_recv, next_recv, sum_send, sum_recv, tot_ref, tot_recv,
    in_sem, k_sem, ex_send, ex_recv, st_send, st_recv, rel_send, rel_recv, sum_ssem, sum_rsem, tot_ssem, tot_rsem,
):
    rows = x0_ref.shape[0]
    me, cs = lax.axis_index("sub"), lax.axis_index("case")
    nxt, prv, part = lax.rem(me + 1, n), lax.rem(me + n - 1, n), lax.rem(me + n // 2, n)
    depth = k_ref.shape[0] // chunks
    per = SLOTS // nc if SLOTS % nc == 0 else SLOTS
    relayed = per < SLOTS
    contact = pl.ds(2 * BLK, SLOTS * BLK)

    k_copies = [
        pltpu.make_async_copy(
            k_hbm.at[pl.ds(i * depth, depth)], k_ref.at[pl.ds(i * depth, depth)], k_sem.at[i]
        )
        for i in range(chunks)
    ]
    x0_copy, b_copy, match_copy, mortar_copy, ids_copy, count_copy = loads = [
        pltpu.make_async_copy(src, dst, in_sem.at[i])
        for i, (src, dst) in enumerate([
            (x0_hbm, x0_ref), (b_hbm, b_ref), (match_hbm, match_ref), (mortar_hbm, mortar_ref),
            (ids_hbm, ids_ref), (count_hbm, count_ref),
        ])
    ]
    for copy in loads + k_copies:
        copy.start()

    barrier = pltpu.get_barrier_semaphore()
    greeted = 0

    def greet(sub, case):
        pl.semaphore_signal(barrier, inc=1, device_id=(sub, case), device_id_type=MESH)

    stride = 1
    rounds = []
    for f in factors:
        digit = lax.rem(me // stride, f)
        base = me - digit * stride
        rounds.append((f, stride, digit, base))
        for j in range(1, f):
            greet(base + lax.rem(digit + j, f) * stride, cs)
            greeted += 1
        stride *= f
    if len(factors) > 1:
        for other in (nxt, prv, part):
            greet(other, cs)
            greeted += 1
    for j in range(1, nc):
        greet(me, lax.rem(cs + j, nc))
        greeted += 1

    x0_copy.wait()
    con_send[0] = x0_ref[:, 2 * BLK:(2 + SLOTS) * BLK].astype(BF16)
    ids_copy.wait()
    count_copy.wait()
    match_copy.wait()
    line = lax.broadcasted_iota(jnp.int32, (1, BLK), 1) * 0
    for k in range(SLOTS):
        for b in range(SLOTS):
            pack_ref[k * SLOTS + b:k * SLOTS + b + 1, :] = jnp.where(line + ids_ref[0, k] == b, 1.0, 0.0)
        live = SLOTS * SLOTS + k
        pack_ref[live:live + 1, :] = jnp.where(line + count_ref[0] > k, 1.0, 0.0)
    pack_ref[SLOTS * SLOTS + SLOTS:, :] = jnp.zeros((SLOTS, BLK), F32)
    lanes = lax.broadcasted_iota(jnp.int32, (BLK, BLK), 0)
    for side in range(2):
        perm_ref[side] = jnp.where(lanes == match_ref[0, side:side + 1, :], 1.0, 0.0).astype(BF16)

    mortar_copy.wait()
    pl.semaphore_wait(barrier, greeted)

    def remote(src, dst, ssem, rsem, sub, case):
        return pltpu.make_async_remote_copy(
            src_ref=src, dst_ref=dst, send_sem=ssem, recv_sem=rsem,
            device_id=(sub, case), device_id_type=MESH,
        )

    def exchange(vec_ref, slot):
        return [
            remote(con_send.at[slot], con_recv.at[slot], ex_send.at[slot, 0], ex_recv.at[slot, 0], part, cs),
            remote(vec_ref.at[:, pl.ds(BLK, BLK)], prev_recv.at[slot], ex_send.at[slot, 1], ex_recv.at[slot, 1], nxt, cs),
            remote(vec_ref.at[:, pl.ds(0, BLK)], next_recv.at[slot], ex_send.at[slot, 2], ex_recv.at[slot, 2], prv, cs),
        ]

    first = exchange(x0_ref, 0)
    mine = pl.ds(cs * per, per) if relayed else pl.ds(0, SLOTS)
    static = [
        remote(pack_ref, pack_p, st_send.at[0], st_recv.at[0], part, cs),
        remote(mortar_ref.at[0, mine], mort_p.at[mine], st_send.at[1], st_recv.at[1], part, cs),
    ]
    for copy in first + static:
        copy.start()

    x_ref[...] = x0_ref[...]
    for i in range(chunks):
        k_copies[i].wait()
        term = jnp.dot(
            x0_ref[:, i * depth:(i + 1) * depth].astype(BF16), k_ref[i * depth:(i + 1) * depth, :],
            preferred_element_type=F32,
        )
        if i == 0:
            kx_ref[...] = term
        else:
            kx_ref[...] += term

    b_copy.wait()
    static[1].wait_recv()
    if relayed:
        relays = []
        for j in range(1, nc):
            copy = remote(mort_p.at[mine], mort_p.at[mine], rel_send.at[j - 1], rel_recv.at[j - 1], me, lax.rem(cs + j, nc))
            copy.start()
            relays.append(copy)

    for copy in first:
        copy.wait()
    static[0].wait()
    sx_ref[0] = times(prev_recv[0], perm_ref[0])
    sx_ref[1] = times(next_recv[0], perm_ref[1])
    xp_ref[...] = con_recv[0].astype(F32)
    static[1].wait_send()
    if relayed:
        for j in range(1, nc):
            from_other = pl.ds(lax.rem(cs + nc - j, nc) * per, per)
            remote(
                mort_p.at[from_other], mort_p.at[from_other], rel_send.at[j - 1], rel_recv.at[j - 1],
                me, lax.rem(cs + j, nc),
            ).wait_recv()
        for copy in relays:
            copy.wait_send()

    row = lax.broadcasted_iota(jnp.int32, (rows, BLK), 0)
    lane = lax.broadcasted_iota(jnp.int32, (rows, BLK), 1)

    def block(value, b):
        return value[:, b * BLK:(b + 1) * BLK]

    def chosen(pack, value, k):
        total = pack[k * SLOTS:k * SLOTS + 1, :] * block(value, 0)
        for b in range(1, SLOTS):
            total += pack[k * SLOTS + b:k * SLOTS + b + 1, :] * block(value, b)
        return total

    def live(pack, k):
        return pack[SLOTS * SLOTS + k:SLOTS * SLOTS + k + 1, :]

    def body(it, carry):
        slot = it + 1
        own, other = pack_ref[...], pack_p[...]
        x, xp = x_ref[:, 2 * BLK:(2 + SLOTS) * BLK], xp_ref[...]
        replies = [jnp.zeros((rows, BLK), F32)] * SLOTS
        for k in range(SLOTS):
            jump_p = (times(chosen(other, x, k), mort_p[k]) - block(xp, k)) * live(other, k)
            back = times(jump_p, mort_p[k], True)
            for b in range(SLOTS):
                replies[b] = replies[b] + other[k * SLOTS + b:k * SLOTS + b + 1, :] * back
        for k in range(SLOTS):
            at = slice((2 + k) * BLK, (3 + k) * BLK)
            jump = (times(chosen(own, xp, k), mortar_ref[0, k]) - block(x, k)) * live(own, k)
            grad = kx_ref[:, at] + (replies[k] - jump) - b_ref[:, at]
            g_ref[:, at] = grad
            con_send[slot, :, k * BLK:(k + 1) * BLK] = grad.astype(BF16)
        for side in range(2):
            at = slice(side * BLK, (side + 1) * BLK)
            g_ref[:, at] = kx_ref[:, at] + PENALTY * (x_ref[:, at] - sx_ref[side]) - b_ref[:, at]
        moved = exchange(g_ref, slot)
        for copy in moved:
            copy.start()
        rest = slice((2 + SLOTS) * BLK, None)
        g_ref[:, rest] = kx_ref[:, rest] - b_ref[:, rest]

        g = g_ref[...]
        q_ref[...] = jnp.dot(g.astype(BF16), k_ref[...], preferred_element_type=F32)
        q = q_ref[...]
        norm = curve = jnp.zeros((rows, BLK), F32)
        for b in range(g.shape[1] // BLK):
            norm += block(g, b) * block(g, b)
            curve += block(g, b) * block(q, b)
        for copy in moved:
            copy.wait()
        sg = [times(prev_recv[slot], perm_ref[0]), times(next_recv[slot], perm_ref[1])]
        for side in range(2):
            curve += PENALTY * block(g, side) * (block(g, side) - sg[side])
        gp = con_recv[slot].astype(F32)
        for k in range(SLOTS):
            image = jnp.dot(chosen(own, gp, k).astype(BF16), mortar_ref[0, k], preferred_element_type=F32)
            jump = (image - block(g, 2 + k)) * live(own, k)
            curve += jump * jump
        norm = jnp.sum(norm, axis=1, keepdims=True)
        curve = jnp.sum(curve, axis=1, keepdims=True)
        packed = jnp.where(lane == row, norm, 0.0) + jnp.where(lane == row + rows, curve, 0.0)
        total = jnp.sum(packed, axis=0, keepdims=True)
        for r, (f, stride, digit, base) in enumerate(rounds):
            sum_send[it, r] = total
            sum_recv[it, r, digit] = total
            sends = []
            for j in range(1, f):
                copy = remote(
                    sum_send.at[it, r], sum_recv.at[it, r, digit], sum_ssem.at[it, r, j], sum_rsem.at[it, r, digit],
                    base + lax.rem(digit + j, f) * stride, cs,
                )
                copy.start()
                sends.append(copy)
            for j in range(1, f):
                source = lax.rem(digit + j, f)
                remote(
                    sum_send.at[it, r], sum_recv.at[it, r, source], sum_ssem.at[it, r, j], sum_rsem.at[it, r, source],
                    base + source * stride, cs,
                ).wait_recv()
            total = sum_recv[it, r, 0]
            for d in range(1, f):
                total = total + sum_recv[it, r, d]
            for copy in sends:
                copy.wait_send()
        tot_ref[...] = total
        wide = jnp.broadcast_to(total, (rows, BLK))
        top = jnp.sum(jnp.where(lane == row, wide, 0.0), axis=1, keepdims=True)
        bottom = jnp.sum(jnp.where(lane == row + rows, wide, 0.0), axis=1, keepdims=True)
        step = top / bottom
        step_wide = jnp.broadcast_to(step, (rows, BLK))

        clipped = []
        for b in range(g.shape[1] // BLK):
            at = slice(b * BLK, (b + 1) * BLK)
            fresh = x_ref[:, at] - step_wide * block(g, b)
            if 2 <= b < 2 + SLOTS:
                kept = jnp.maximum(fresh, 0.0)
                clipped.append((kept - fresh).astype(BF16))
                fresh = kept
            x_ref[:, at] = fresh
        for k in range(SLOTS):
            at = slice(k * BLK, (k + 1) * BLK)
            xp_ref[:, at] = jnp.maximum(xp_ref[:, at] - step_wide * block(gp, k), 0.0)
        for side in range(2):
            sx_ref[side] = sx_ref[side] - step_wide * sg[side]

        @pl.when(it < ITERS - 1)
        def _():
            pushed = jnp.dot(
                jnp.concatenate(clipped, axis=1), k_ref[2 * BLK:(2 + SLOTS) * BLK, :], preferred_element_type=F32
            )
            for b in range(g.shape[1] // BLK):
                at = slice(b * BLK, (b + 1) * BLK)
                kx_ref[:, at] = kx_ref[:, at] - step_wide * q_ref[:, at] + block(pushed, b)

        return carry

    lax.fori_loop(0, ITERS, body, 0)

    tot_recv[cs] = tot_ref[...]
    sends = []
    for j in range(1, nc):
        copy = remote(tot_ref, tot_recv.at[cs], tot_ssem.at[j], tot_rsem.at[cs], me, lax.rem(cs + j, nc))
        copy.start()
        sends.append(copy)
    out_ref[...] = x_ref[...]
    for j in range(1, nc):
        source = lax.rem(cs + j, nc)
        remote(tot_ref, tot_recv.at[source], tot_ssem.at[j], tot_rsem.at[source], me, source).wait_recv()
    for copy in sends:
        copy.wait_send()
    total = tot_recv[0]
    for d in range(1, nc):
        total = total + tot_recv[d]
    flat = lax.broadcasted_iota(jnp.int32, (1, BLK), 1)
    whole = jnp.sum(jnp.where(flat < rows, total, 0.0), axis=1, keepdims=True)
    norm_ref[0] = jnp.sqrt(whole)[0, 0]


def solution(mesh):
    n, nc = mesh.shape["sub"], mesh.shape["case"]
    factors = radices(n)
    chunks = 3

    def on_device(multipliers, right_side, dual_ops, glue_match, mortar, contact_ids, contact_count):
        rows, order = multipliers.shape
        top = max(factors)
        rounds = len(factors)
        vmem = pl.BlockSpec(memory_space=pltpu.VMEM)
        smem = pl.BlockSpec(memory_space=pltpu.SMEM)
        dma = pltpu.SemaphoreType.DMA
        slots = ITERS + 1
        return pl.pallas_call(
            functools.partial(kernel, n, nc, factors, chunks),
            out_shape=(
                jax.ShapeDtypeStruct((rows, order), F32),
                jax.ShapeDtypeStruct((1,), F32),
            ),
            in_specs=[pl.BlockSpec(memory_space=pltpu.HBM)] * 7,
            out_specs=(vmem, smem),
            scratch_shapes=[
                pltpu.VMEM((rows, order), F32),
                pltpu.VMEM((rows, order), F32),
                pltpu.VMEM(glue_match.shape, jnp.int32),
                pltpu.VMEM(mortar.shape, BF16),
                pltpu.SMEM(contact_ids.shape, jnp.int32),
                pltpu.SMEM(contact_count.shape, jnp.int32),
                pltpu.VMEM((order, order), BF16),
                pltpu.VMEM((rows, order), F32),
                pltpu.VMEM((rows, order), F32),
                pltpu.VMEM((rows, order), F32),
                pltpu.VMEM((rows, order), F32),
                pltpu.VMEM((2, rows, BLK), F32),
                pltpu.VMEM((rows, SLOTS * BLK), F32),
                pltpu.VMEM((2, BLK, BLK), BF16),
                pltpu.VMEM((SLOTS * SLOTS + 2 * SLOTS, BLK), F32),
                pltpu.VMEM((SLOTS * SLOTS + 2 * SLOTS, BLK), F32),
                pltpu.VMEM((SLOTS, BLK, BLK), BF16),
                pltpu.VMEM((slots, rows, SLOTS * BLK), BF16),
                pltpu.VMEM((slots, rows, SLOTS * BLK), BF16),
                pltpu.VMEM((slots, rows, BLK), F32),
                pltpu.VMEM((slots, rows, BLK), F32),
                pltpu.VMEM((ITERS, rounds, 1, BLK), F32),
                pltpu.VMEM((ITERS, rounds, top, 1, BLK), F32),
                pltpu.VMEM((1, BLK), F32),
                pltpu.VMEM((nc, 1, BLK), F32),
                dma((6,)),
                dma((chunks,)),
                dma((slots, 3)),
                dma((slots, 3)),
                dma((2,)),
                dma((2,)),
                dma((max(nc - 1, 1),)),
                dma((max(nc - 1, 1),)),
                dma((ITERS, rounds, top)),
                dma((ITERS, rounds, top)),
                dma((nc,)),
                dma((nc,)),
            ],
            compiler_params=pltpu.CompilerParams(
                collective_id=0, has_side_effects=True, vmem_limit_bytes=58 * 1024 * 1024
            ),
        )(multipliers, right_side, dual_ops, glue_match, mortar, contact_ids, contact_count)

    in_specs = (
        P("case", "sub"),
        P("case", "sub"),
        P("sub", None),
        P("sub", None, None),
        P("sub", None, None, None),
        P("sub", None),
        P("sub"),
    )
    return jax.shard_map(
        on_device, mesh=mesh, in_specs=in_specs, out_specs=(P("case", "sub"), P()), check_vma=False
    )
```

```python
import functools

import jax
import jax.numpy as jnp
from jax import lax
from jax.experimental import pallas as pl
from jax.experimental.pallas import tpu as pltpu
from jax.sharding import PartitionSpec as P

ITERS = 4
BLK = 128
SLOTS = 4
PENALTY = 0.5
MESH = pl.DeviceIdType.MESH
F32 = jnp.float32
BF16 = jnp.bfloat16


def radices(count):
    out = []
    while count > 1:
        factor = next(f for f in (8, 7, 6, 5, 4, 3, 2, count) if count % f == 0)
        out.append(factor)
        count //= factor
    return out


def halves(value):
    high = value.astype(BF16)
    low = (value - high.astype(F32)).astype(BF16)
    return jnp.concatenate([high, low], axis=0)


def times(value, weight, transposed=False):
    rows = value.shape[0]
    dims = (((1,), (1 if transposed else 0,)), ((), ()))
    both = lax.dot_general(halves(value), weight, dims, preferred_element_type=F32)
    return both[:rows] + both[rows:]


def kernel(
    n, nc, factors, chunks,
    x0_hbm, b_hbm, k_hbm, match_hbm, mortar_hbm, ids_hbm, count_hbm,
    out_ref, norm_ref,
    x0_ref, b_ref, match_ref, mortar_ref, ids_ref, count_ref,
    k_ref, x_ref, g_ref, kx_ref, q_ref, sx_ref, xp_ref, perm_ref, pack_ref, pack_p, mort_p,
    con_send, con_recv, prev_recv, next_recv, cross_ref, mid_perm, mid_tail, mid_head, sum_send, sum_recv, tot_ref, tot_recv,
    in_sem, k_sem, ex_send, ex_recv, st_send, st_recv, rel_send, rel_recv, sum_ssem, sum_rsem, tot_ssem, tot_rsem,
    mid_send, mid_recv,
):
    rows = x0_ref.shape[0]
    me, cs = lax.axis_index("sub"), lax.axis_index("case")
    nxt, prv, part = lax.rem(me + 1, n), lax.rem(me + n - 1, n), lax.rem(me + n // 2, n)
    depth = k_ref.shape[0] // chunks
    per = SLOTS // nc if SLOTS % nc == 0 else SLOTS
    relayed = per < SLOTS
    contact = pl.ds(2 * BLK, SLOTS * BLK)

    halfway = len(factors) == 1 and n >= 4
    middle, last = n // 2 - 1, n - 1
    direct = me != 0 if halfway else me >= 0

    k_copies = [
        pltpu.make_async_copy(
            k_hbm.at[pl.ds(i * depth, depth)], k_ref.at[pl.ds(i * depth, depth)], k_sem.at[i]
        )
        for i in range(chunks)
    ]
    x0_copy, b_copy, match_copy, mortar_copy, ids_copy, count_copy = loads = [
        pltpu.make_async_copy(src, dst, in_sem.at[i])
        for i, (src, dst) in enumerate([
            (x0_hbm, x0_ref), (b_hbm, b_ref), (match_hbm, match_ref), (mortar_hbm, mortar_ref),
            (ids_hbm, ids_ref), (count_hbm, count_ref),
        ])
    ]
    for copy in loads + k_copies:
        copy.start()

    barrier = pltpu.get_barrier_semaphore()
    greeted = 0

    def greet(sub, case):
        pl.semaphore_signal(barrier, inc=1, device_id=(sub, case), device_id_type=MESH)

    stride = 1
    rounds = []
    for f in factors:
        digit = lax.rem(me // stride, f)
        base = me - digit * stride
        rounds.append((f, stride, digit, base))
        for j in range(1, f):
            greet(base + lax.rem(digit + j, f) * stride, cs)
            greeted += 1
        stride *= f
    if len(factors) > 1:
        for other in (nxt, prv, part):
            greet(other, cs)
            greeted += 1
    for j in range(1, nc):
        greet(me, lax.rem(cs + j, nc))
        greeted += 1

    x0_copy.wait()
    con_send[0] = x0_ref[:, 2 * BLK:(2 + SLOTS) * BLK].astype(BF16)
    ids_copy.wait()
    count_copy.wait()
    match_copy.wait()
    line = lax.broadcasted_iota(jnp.int32, (1, BLK), 1) * 0
    for k in range(SLOTS):
        for b in range(SLOTS):
            pack_ref[k * SLOTS + b:k * SLOTS + b + 1, :] = jnp.where(line + ids_ref[0, k] == b, 1.0, 0.0)
        live = SLOTS * SLOTS + k
        pack_ref[live:live + 1, :] = jnp.where(line + count_ref[0] > k, 1.0, 0.0)
    pack_ref[SLOTS * SLOTS + SLOTS:, :] = jnp.zeros((SLOTS, BLK), F32)
    lanes = lax.broadcasted_iota(jnp.int32, (BLK, BLK), 0)
    for side in range(2):
        perm_ref[side] = jnp.where(lanes == match_ref[0, side:side + 1, :], 1.0, 0.0).astype(BF16)

    mortar_copy.wait()
    pl.semaphore_wait(barrier, greeted)

    def remote(src, dst, ssem, rsem, sub, case):
        return pltpu.make_async_remote_copy(
            src_ref=src, dst_ref=dst, send_sem=ssem, recv_sem=rsem,
            device_id=(sub, case), device_id_type=MESH,
        )

    def exchange(vec_ref, slot):
        return [
            remote(con_send.at[slot], con_recv.at[slot], ex_send.at[slot, 0], ex_recv.at[slot, 0], part, cs),
            remote(vec_ref.at[:, pl.ds(BLK, BLK)], prev_recv.at[slot], ex_send.at[slot, 1], ex_recv.at[slot, 1], nxt, cs),
            remote(vec_ref.at[:, pl.ds(0, BLK)], next_recv.at[slot], ex_send.at[slot, 2], ex_recv.at[slot, 2], prv, cs),
        ]

    first = exchange(x0_ref, 0)
    mine = pl.ds(cs * per, per) if relayed else pl.ds(0, SLOTS)
    static = [
        remote(pack_ref, pack_p, st_send.at[0], st_recv.at[0], part, cs),
        remote(mortar_ref.at[0, mine], mort_p.at[mine], st_send.at[1], st_recv.at[1], part, cs),
    ]
    for copy in first + static:
        copy.start()

    def mid_static():
        return remote(perm_ref.at[0], mid_perm, mid_send.at[0], mid_recv.at[0], middle, cs)

    def mid_first(slot):
        return remote(g_ref.at[:, pl.ds(0, BLK)], mid_head.at[slot], mid_send.at[1], mid_recv.at[1 + slot], middle, cs)

    def mid_last(slot):
        return remote(
            g_ref.at[:, pl.ds(BLK, BLK)], mid_tail.at[slot], mid_send.at[2], mid_recv.at[1 + ITERS + slot], middle, cs
        )

    if halfway:
        @pl.when(me == 0)
        def _():
            mid_static().start()

    x_ref[...] = x0_ref[...]
    for i in range(chunks):
        k_copies[i].wait()
        term = jnp.dot(
            x0_ref[:, i * depth:(i + 1) * depth].astype(BF16), k_ref[i * depth:(i + 1) * depth, :],
            preferred_element_type=F32,
        )
        if i == 0:
            kx_ref[...] = term
        else:
            kx_ref[...] += term

    b_copy.wait()
    static[1].wait_recv()
    if relayed:
        relays = []
        for j in range(1, nc):
            copy = remote(mort_p.at[mine], mort_p.at[mine], rel_send.at[j - 1], rel_recv.at[j - 1], me, lax.rem(cs + j, nc))
            copy.start()
            relays.append(copy)

    for copy in first:
        copy.wait()
    static[0].wait()
    sx_ref[0] = times(prev_recv[0], perm_ref[0])
    sx_ref[1] = times(next_recv[0], perm_ref[1])
    xp_ref[...] = con_recv[0].astype(F32)
    static[1].wait_send()
    if relayed:
        for j in range(1, nc):
            from_other = pl.ds(lax.rem(cs + nc - j, nc) * per, per)
            remote(
                mort_p.at[from_other], mort_p.at[from_other], rel_send.at[j - 1], rel_recv.at[j - 1],
                me, lax.rem(cs + j, nc),
            ).wait_recv()
        for copy in relays:
            copy.wait_send()

    if halfway:
        @pl.when(me == 0)
        def _():
            mid_static().wait_send()

        @pl.when(me == middle)
        def _():
            mid_static_in = pltpu.make_async_remote_copy(
                src_ref=perm_ref.at[0], dst_ref=mid_perm, send_sem=mid_send.at[0], recv_sem=mid_recv.at[0],
                device_id=(0, cs), device_id_type=MESH,
            )
            mid_static_in.wait_recv()

    row = lax.broadcasted_iota(jnp.int32, (rows, BLK), 0)
    lane = lax.broadcasted_iota(jnp.int32, (rows, BLK), 1)

    def block(value, b):
        return value[:, b * BLK:(b + 1) * BLK]

    def chosen(pack, value, k):
        total = pack[k * SLOTS:k * SLOTS + 1, :] * block(value, 0)
        for b in range(1, SLOTS):
            total += pack[k * SLOTS + b:k * SLOTS + b + 1, :] * block(value, b)
        return total

    def live(pack, k):
        return pack[SLOTS * SLOTS + k:SLOTS * SLOTS + k + 1, :]

    def body(it, carry):
        slot = it + 1
        own, other = pack_ref[...], pack_p[...]
        x, xp = x_ref[:, 2 * BLK:(2 + SLOTS) * BLK], xp_ref[...]
        replies = [jnp.zeros((rows, BLK), F32)] * SLOTS
        for k in range(SLOTS):
            jump_p = (times(chosen(other, x, k), mort_p[k]) - block(xp, k)) * live(other, k)
            back = times(jump_p, mort_p[k], True)
            for b in range(SLOTS):
                replies[b] = replies[b] + other[k * SLOTS + b:k * SLOTS + b + 1, :] * back
        for k in range(SLOTS):
            at = slice((2 + k) * BLK, (3 + k) * BLK)
            jump = (times(chosen(own, xp, k), mortar_ref[0, k]) - block(x, k)) * live(own, k)
            grad = kx_ref[:, at] + (replies[k] - jump) - b_ref[:, at]
            g_ref[:, at] = grad
            con_send[slot, :, k * BLK:(k + 1) * BLK] = grad.astype(BF16)
        for side in range(2):
            at = slice(side * BLK, (side + 1) * BLK)
            g_ref[:, at] = kx_ref[:, at] + PENALTY * (x_ref[:, at] - sx_ref[side]) - b_ref[:, at]
        moved = exchange(g_ref, slot)
        if halfway:
            @pl.when(me == 0)
            def _():
                mid_first(it).start()

            @pl.when(me == last)
            def _():
                mid_last(it).start()
        for copy in moved:
            copy.start()
        rest = slice((2 + SLOTS) * BLK, None)
        g_ref[:, rest] = kx_ref[:, rest] - b_ref[:, rest]

        g = g_ref[...]
        q_ref[...] = jnp.dot(g.astype(BF16), k_ref[...], preferred_element_type=F32)
        q = q_ref[...]
        norm = curve = jnp.zeros((rows, BLK), F32)
        for b in range(g.shape[1] // BLK):
            norm += block(g, b) * block(g, b)
            curve += block(g, b) * block(q, b)
        for side in range(2):
            curve += PENALTY * block(g, side) * block(g, side)
        cross_ref[...] = jnp.zeros((rows, BLK), F32)

        @pl.when(direct)
        def _():
            moved[1].wait_recv()
            cross_ref[...] = g_ref[:, :BLK] * times(prev_recv[slot], perm_ref[0])

        if halfway:
            @pl.when(me == middle)
            def _():
                for sem, dst, sub in ((1 + it, mid_head, 0), (1 + ITERS + it, mid_tail, last)):
                    pltpu.make_async_remote_copy(
                        src_ref=g_ref.at[:, pl.ds(0, BLK)], dst_ref=dst.at[it], send_sem=mid_send.at[1],
                        recv_sem=mid_recv.at[sem], device_id=(sub, cs), device_id_type=MESH,
                    ).wait_recv()
                cross_ref[...] += mid_head[it] * times(mid_tail[it], mid_perm[...])

        moved[0].wait_recv()
        curve = curve - cross_ref[...]
        gp = con_recv[slot].astype(F32)
        for k in range(SLOTS):
            image = jnp.dot(chosen(own, gp, k).astype(BF16), mortar_ref[0, k], preferred_element_type=F32)
            jump = (image - block(g, 2 + k)) * live(own, k)
            curve += jump * jump
        norm = jnp.sum(norm, axis=1, keepdims=True)
        curve = jnp.sum(curve, axis=1, keepdims=True)
        packed = jnp.where(lane == row, norm, 0.0) + jnp.where(lane == row + rows, curve, 0.0)
        total = jnp.sum(packed, axis=0, keepdims=True)
        for r, (f, stride, digit, base) in enumerate(rounds):
            sum_send[it, r] = total
            sum_recv[it, r, digit] = total
            sends = []
            for j in sorted(range(1, f), key=lambda j: abs(2 * j - f)):
                copy = remote(
                    sum_send.at[it, r], sum_recv.at[it, r, digit], sum_ssem.at[it, r, j], sum_rsem.at[it, r, digit],
                    base + lax.rem(digit + j, f) * stride, cs,
                )
                copy.start()
                sends.append(copy)
            for j in range(1, f):
                source = lax.rem(digit + j, f)
                remote(
                    sum_send.at[it, r], sum_recv.at[it, r, source], sum_ssem.at[it, r, j], sum_rsem.at[it, r, source],
                    base + source * stride, cs,
                ).wait_recv()
            total = sum_recv[it, r, 0]
            for d in range(1, f):
                total = total + sum_recv[it, r, d]
            for copy in sends:
                copy.wait_send()
        tot_ref[...] = total
        if halfway:
            @pl.when(me == 0)
            def _():
                moved[1].wait_recv()
                mid_first(it).wait_send()

            @pl.when(me == last)
            def _():
                mid_last(it).wait_send()
        moved[2].wait_recv()
        for copy in moved:
            copy.wait_send()
        sg = [times(prev_recv[slot], perm_ref[0]), times(next_recv[slot], perm_ref[1])]
        wide = jnp.broadcast_to(total, (rows, BLK))
        top = jnp.sum(jnp.where(lane == row, wide, 0.0), axis=1, keepdims=True)
        bottom = jnp.sum(jnp.where(lane == row + rows, wide, 0.0), axis=1, keepdims=True)
        step = top / bottom
        step_wide = jnp.broadcast_to(step, (rows, BLK))

        clipped = []
        for b in range(g.shape[1] // BLK):
            at = slice(b * BLK, (b + 1) * BLK)
            fresh = x_ref[:, at] - step_wide * block(g, b)
            if 2 <= b < 2 + SLOTS:
                kept = jnp.maximum(fresh, 0.0)
                clipped.append((kept - fresh).astype(BF16))
                fresh = kept
            x_ref[:, at] = fresh
        for k in range(SLOTS):
            at = slice(k * BLK, (k + 1) * BLK)
            xp_ref[:, at] = jnp.maximum(xp_ref[:, at] - step_wide * block(gp, k), 0.0)
        for side in range(2):
            sx_ref[side] = sx_ref[side] - step_wide * sg[side]

        @pl.when(it < ITERS - 1)
        def _():
            pushed = jnp.dot(
                jnp.concatenate(clipped, axis=1), k_ref[2 * BLK:(2 + SLOTS) * BLK, :], preferred_element_type=F32
            )
            for b in range(g.shape[1] // BLK):
                at = slice(b * BLK, (b + 1) * BLK)
                kx_ref[:, at] = kx_ref[:, at] - step_wide * q_ref[:, at] + block(pushed, b)

        return carry

    lax.fori_loop(0, ITERS, body, 0)

    tot_recv[cs] = tot_ref[...]
    sends = []
    for j in range(1, nc):
        copy = remote(tot_ref, tot_recv.at[cs], tot_ssem.at[j], tot_rsem.at[cs], me, lax.rem(cs + j, nc))
        copy.start()
        sends.append(copy)
    out_ref[...] = x_ref[...]
    for j in range(1, nc):
        source = lax.rem(cs + j, nc)
        remote(tot_ref, tot_recv.at[source], tot_ssem.at[j], tot_rsem.at[source], me, source).wait_recv()
    for copy in sends:
        copy.wait_send()
    total = tot_recv[0]
    for d in range(1, nc):
        total = total + tot_recv[d]
    flat = lax.broadcasted_iota(jnp.int32, (1, BLK), 1)
    whole = jnp.sum(jnp.where(flat < rows, total, 0.0), axis=1, keepdims=True)
    norm_ref[0] = jnp.sqrt(whole)[0, 0]


def solution(mesh):
    n, nc = mesh.shape["sub"], mesh.shape["case"]
    factors = radices(n)
    chunks = 3

    def on_device(multipliers, right_side, dual_ops, glue_match, mortar, contact_ids, contact_count):
        rows, order = multipliers.shape
        top = max(factors)
        rounds = len(factors)
        vmem = pl.BlockSpec(memory_space=pltpu.VMEM)
        smem = pl.BlockSpec(memory_space=pltpu.SMEM)
        dma = pltpu.SemaphoreType.DMA
        slots = ITERS + 1
        return pl.pallas_call(
            functools.partial(kernel, n, nc, factors, chunks),
            out_shape=(
                jax.ShapeDtypeStruct((rows, order), F32),
                jax.ShapeDtypeStruct((1,), F32),
            ),
            in_specs=[pl.BlockSpec(memory_space=pltpu.HBM)] * 7,
            out_specs=(vmem, smem),
            scratch_shapes=[
                pltpu.VMEM((rows, order), F32),
                pltpu.VMEM((rows, order), F32),
                pltpu.VMEM(glue_match.shape, jnp.int32),
                pltpu.VMEM(mortar.shape, BF16),
                pltpu.SMEM(contact_ids.shape, jnp.int32),
                pltpu.SMEM(contact_count.shape, jnp.int32),
                pltpu.VMEM((order, order), BF16),
                pltpu.VMEM((rows, order), F32),
                pltpu.VMEM((rows, order), F32),
                pltpu.VMEM((rows, order), F32),
                pltpu.VMEM((rows, order), F32),
                pltpu.VMEM((2, rows, BLK), F32),
                pltpu.VMEM((rows, SLOTS * BLK), F32),
                pltpu.VMEM((2, BLK, BLK), BF16),
                pltpu.VMEM((SLOTS * SLOTS + 2 * SLOTS, BLK), F32),
                pltpu.VMEM((SLOTS * SLOTS + 2 * SLOTS, BLK), F32),
                pltpu.VMEM((SLOTS, BLK, BLK), BF16),
                pltpu.VMEM((slots, rows, SLOTS * BLK), BF16),
                pltpu.VMEM((slots, rows, SLOTS * BLK), BF16),
                pltpu.VMEM((slots, rows, BLK), F32),
                pltpu.VMEM((slots, rows, BLK), F32),
                pltpu.VMEM((rows, BLK), F32),
                pltpu.VMEM((BLK, BLK), BF16),
                pltpu.VMEM((ITERS, rows, BLK), F32),
                pltpu.VMEM((ITERS, rows, BLK), F32),
                pltpu.VMEM((ITERS, rounds, 1, BLK), F32),
                pltpu.VMEM((ITERS, rounds, top, 1, BLK), F32),
                pltpu.VMEM((1, BLK), F32),
                pltpu.VMEM((nc, 1, BLK), F32),
                dma((6,)),
                dma((chunks,)),
                dma((slots, 3)),
                dma((slots, 3)),
                dma((2,)),
                dma((2,)),
                dma((max(nc - 1, 1),)),
                dma((max(nc - 1, 1),)),
                dma((ITERS, rounds, top)),
                dma((ITERS, rounds, top)),
                dma((nc,)),
                dma((nc,)),
                dma((3,)),
                dma((1 + 2 * ITERS,)),
            ],
            compiler_params=pltpu.CompilerParams(
                collective_id=0, has_side_effects=True, vmem_limit_bytes=58 * 1024 * 1024
            ),
        )(multipliers, right_side, dual_ops, glue_match, mortar, contact_ids, contact_count)

    in_specs = (
        P("case", "sub"),
        P("case", "sub"),
        P("sub", None),
        P("sub", None, None),
        P("sub", None, None, None),
        P("sub", None),
        P("sub"),
    )
    return jax.shard_map(
        on_device, mesh=mesh, in_specs=in_specs, out_specs=(P("case", "sub"), P()), check_vma=False
    )
```

```python
import functools

import jax
import jax.numpy as jnp
from jax import lax
from jax.experimental import pallas as pl
from jax.experimental.pallas import tpu as pltpu
from jax.sharding import PartitionSpec as P

ITERS = 4
BLK = 128
SLOTS = 4
PENALTY = 0.5
MESH = pl.DeviceIdType.MESH
F32 = jnp.float32
BF16 = jnp.bfloat16


def radices(count):
    out = []
    while count > 1:
        factor = next(f for f in (8, 7, 6, 5, 4, 3, 2, count) if count % f == 0)
        out.append(factor)
        count //= factor
    return out


def halves(value):
    high = value.astype(BF16)
    low = (value - high.astype(F32)).astype(BF16)
    return jnp.concatenate([high, low], axis=0)


def times(value, weight, transposed=False):
    rows = value.shape[0]
    dims = (((1,), (1 if transposed else 0,)), ((), ()))
    both = lax.dot_general(halves(value), weight, dims, preferred_element_type=F32)
    return both[:rows] + both[rows:]


def kernel(
    n, nc, factors, chunks,
    x0_hbm, b_hbm, k_hbm, match_hbm, mortar_hbm, ids_hbm, count_hbm,
    out_ref, norm_ref,
    x0_ref, b_ref, match_ref, mortar_ref, ids_ref, count_ref,
    k_ref, x_ref, g_ref, kx_ref, q_ref, sx_ref, xp_ref, perm_ref, pack_ref, pack_p, mort_p,
    con_send, con_recv, prev_recv, next_recv, cross_ref, mid_perm, mid_tail, mid_head, sum_send, sum_recv, tot_ref, tot_recv,
    in_sem, k_sem, ex_send, ex_recv, st_send, st_recv, rel_send, rel_recv, sum_ssem, sum_rsem, tot_ssem, tot_rsem,
    mid_send, mid_recv,
):
    rows = x0_ref.shape[0]
    me, cs = lax.axis_index("sub"), lax.axis_index("case")
    nxt, prv, part = lax.rem(me + 1, n), lax.rem(me + n - 1, n), lax.rem(me + n // 2, n)
    depth = k_ref.shape[0] // chunks
    per = SLOTS // nc if SLOTS % nc == 0 else SLOTS
    relayed = per < SLOTS
    contact = pl.ds(2 * BLK, SLOTS * BLK)

    halfway = len(factors) == 1 and n >= 4
    middle, last = n // 2 - 1, n - 1
    direct = me != 0 if halfway else me >= 0

    k_copies = [
        pltpu.make_async_copy(
            k_hbm.at[pl.ds(i * depth, depth)], k_ref.at[pl.ds(i * depth, depth)], k_sem.at[i]
        )
        for i in range(chunks)
    ]
    x0_copy, b_copy, match_copy, mortar_copy, ids_copy, count_copy = loads = [
        pltpu.make_async_copy(src, dst, in_sem.at[i])
        for i, (src, dst) in enumerate([
            (x0_hbm, x0_ref), (b_hbm, b_ref), (match_hbm, match_ref), (mortar_hbm, mortar_ref),
            (ids_hbm, ids_ref), (count_hbm, count_ref),
        ])
    ]
    for copy in loads + k_copies:
        copy.start()

    barrier = pltpu.get_barrier_semaphore()
    greeted = 0

    def greet(sub, case):
        pl.semaphore_signal(barrier, inc=1, device_id=(sub, case), device_id_type=MESH)

    stride = 1
    rounds = []
    for f in factors:
        digit = lax.rem(me // stride, f)
        base = me - digit * stride
        rounds.append((f, stride, digit, base))
        for j in range(1, f):
            greet(base + lax.rem(digit + j, f) * stride, cs)
            greeted += 1
        stride *= f
    if len(factors) > 1:
        for other in (nxt, prv, part):
            greet(other, cs)
            greeted += 1
    for j in range(1, nc):
        greet(me, lax.rem(cs + j, nc))
        greeted += 1

    x0_copy.wait()
    con_send[0] = x0_ref[:, 2 * BLK:(2 + SLOTS) * BLK].astype(BF16)
    ids_copy.wait()
    count_copy.wait()
    match_copy.wait()
    line = lax.broadcasted_iota(jnp.int32, (1, BLK), 1) * 0
    for k in range(SLOTS):
        for b in range(SLOTS):
            pack_ref[k * SLOTS + b:k * SLOTS + b + 1, :] = jnp.where(line + ids_ref[0, k] == b, 1.0, 0.0)
        live = SLOTS * SLOTS + k
        pack_ref[live:live + 1, :] = jnp.where(line + count_ref[0] > k, 1.0, 0.0)
    pack_ref[SLOTS * SLOTS + SLOTS:, :] = jnp.zeros((SLOTS, BLK), F32)
    lanes = lax.broadcasted_iota(jnp.int32, (BLK, BLK), 0)
    for side in range(2):
        perm_ref[side] = jnp.where(lanes == match_ref[0, side:side + 1, :], 1.0, 0.0).astype(BF16)

    mortar_copy.wait()
    pl.semaphore_wait(barrier, greeted)

    def remote(src, dst, ssem, rsem, sub, case):
        return pltpu.make_async_remote_copy(
            src_ref=src, dst_ref=dst, send_sem=ssem, recv_sem=rsem,
            device_id=(sub, case), device_id_type=MESH,
        )

    def exchange(vec_ref, slot):
        return [
            remote(con_send.at[slot], con_recv.at[slot], ex_send.at[slot, 0], ex_recv.at[slot, 0], part, cs),
            remote(vec_ref.at[:, pl.ds(BLK, BLK)], prev_recv.at[slot], ex_send.at[slot, 1], ex_recv.at[slot, 1], nxt, cs),
            remote(vec_ref.at[:, pl.ds(0, BLK)], next_recv.at[slot], ex_send.at[slot, 2], ex_recv.at[slot, 2], prv, cs),
        ]

    first = exchange(x0_ref, 0)
    mine = pl.ds(cs * per, per) if relayed else pl.ds(0, SLOTS)
    static = [
        remote(pack_ref, pack_p, st_send.at[0], st_recv.at[0], part, cs),
        remote(mortar_ref.at[0, mine], mort_p.at[mine], st_send.at[1], st_recv.at[1], part, cs),
    ]
    for copy in first + static:
        copy.start()

    def mid_static():
        return remote(perm_ref.at[0], mid_perm, mid_send.at[0], mid_recv.at[0], middle, cs)

    def mid_first(slot):
        return remote(g_ref.at[:, pl.ds(0, BLK)], mid_head.at[slot], mid_send.at[1], mid_recv.at[1 + slot], middle, cs)

    def mid_last(slot):
        return remote(
            g_ref.at[:, pl.ds(BLK, BLK)], mid_tail.at[slot], mid_send.at[2], mid_recv.at[1 + ITERS + slot], middle, cs
        )

    if halfway:
        @pl.when(me == 0)
        def _():
            mid_static().start()

    x_ref[...] = x0_ref[...]
    for i in range(chunks):
        k_copies[i].wait()
        term = jnp.dot(
            x0_ref[:, i * depth:(i + 1) * depth].astype(BF16), k_ref[i * depth:(i + 1) * depth, :],
            preferred_element_type=F32,
        )
        if i == 0:
            kx_ref[...] = term
        else:
            kx_ref[...] += term

    b_copy.wait()
    static[1].wait_recv()
    if relayed:
        relays = []
        for j in range(1, nc):
            copy = remote(mort_p.at[mine], mort_p.at[mine], rel_send.at[j - 1], rel_recv.at[j - 1], me, lax.rem(cs + j, nc))
            copy.start()
            relays.append(copy)

    for copy in first:
        copy.wait()
    static[0].wait()
    sx_ref[0] = times(prev_recv[0], perm_ref[0])
    sx_ref[1] = times(next_recv[0], perm_ref[1])
    xp_ref[...] = con_recv[0].astype(F32)
    static[1].wait_send()
    if relayed:
        for j in range(1, nc):
            from_other = pl.ds(lax.rem(cs + nc - j, nc) * per, per)
            remote(
                mort_p.at[from_other], mort_p.at[from_other], rel_send.at[j - 1], rel_recv.at[j - 1],
                me, lax.rem(cs + j, nc),
            ).wait_recv()
        for copy in relays:
            copy.wait_send()

    if halfway:
        @pl.when(me == 0)
        def _():
            mid_static().wait_send()

        @pl.when(me == middle)
        def _():
            mid_static_in = pltpu.make_async_remote_copy(
                src_ref=perm_ref.at[0], dst_ref=mid_perm, send_sem=mid_send.at[0], recv_sem=mid_recv.at[0],
                device_id=(0, cs), device_id_type=MESH,
            )
            mid_static_in.wait_recv()

    row = lax.broadcasted_iota(jnp.int32, (rows, BLK), 0)
    lane = lax.broadcasted_iota(jnp.int32, (rows, BLK), 1)

    def block(value, b):
        return value[:, b * BLK:(b + 1) * BLK]

    def chosen(pack, value, k):
        total = pack[k * SLOTS:k * SLOTS + 1, :] * block(value, 0)
        for b in range(1, SLOTS):
            total += pack[k * SLOTS + b:k * SLOTS + b + 1, :] * block(value, b)
        return total

    def live(pack, k):
        return pack[SLOTS * SLOTS + k:SLOTS * SLOTS + k + 1, :]

    def to_cases():
        return [
            remote(tot_ref, tot_recv.at[cs], tot_ssem.at[j], tot_rsem.at[cs], me, lax.rem(cs + j, nc))
            for j in range(1, nc)
        ]

    def body(it, carry):
        slot = it + 1
        own, other = pack_ref[...], pack_p[...]
        x, xp = x_ref[:, 2 * BLK:(2 + SLOTS) * BLK], xp_ref[...]
        replies = [jnp.zeros((rows, BLK), F32)] * SLOTS
        for k in range(SLOTS):
            jump_p = (times(chosen(other, x, k), mort_p[k]) - block(xp, k)) * live(other, k)
            back = times(jump_p, mort_p[k], True)
            for b in range(SLOTS):
                replies[b] = replies[b] + other[k * SLOTS + b:k * SLOTS + b + 1, :] * back
        for k in range(SLOTS):
            at = slice((2 + k) * BLK, (3 + k) * BLK)
            jump = (times(chosen(own, xp, k), mortar_ref[0, k]) - block(x, k)) * live(own, k)
            grad = kx_ref[:, at] + (replies[k] - jump) - b_ref[:, at]
            g_ref[:, at] = grad
            con_send[slot, :, k * BLK:(k + 1) * BLK] = grad.astype(BF16)
        moved = exchange(g_ref, slot)
        moved[0].start()
        for side in range(2):
            at = slice(side * BLK, (side + 1) * BLK)
            g_ref[:, at] = kx_ref[:, at] + PENALTY * (x_ref[:, at] - sx_ref[side]) - b_ref[:, at]
        if halfway:
            @pl.when(me == 0)
            def _():
                mid_first(it).start()

            @pl.when(me == last)
            def _():
                mid_last(it).start()
        moved[1].start()
        moved[2].start()
        rest = slice((2 + SLOTS) * BLK, None)
        g_ref[:, rest] = kx_ref[:, rest] - b_ref[:, rest]

        g = g_ref[...]
        q_ref[...] = jnp.dot(g.astype(BF16), k_ref[...], preferred_element_type=F32)
        q = q_ref[...]
        norm = curve = jnp.zeros((rows, BLK), F32)
        for b in range(g.shape[1] // BLK):
            norm += block(g, b) * block(g, b)
            curve += block(g, b) * block(q, b)
        for side in range(2):
            curve += PENALTY * block(g, side) * block(g, side)
        cross_ref[...] = jnp.zeros((rows, BLK), F32)

        @pl.when(direct)
        def _():
            moved[1].wait_recv()
            cross_ref[...] = g_ref[:, :BLK] * times(prev_recv[slot], perm_ref[0])

        if halfway:
            @pl.when(me == middle)
            def _():
                for sem, dst, sub in ((1 + it, mid_head, 0), (1 + ITERS + it, mid_tail, last)):
                    pltpu.make_async_remote_copy(
                        src_ref=g_ref.at[:, pl.ds(0, BLK)], dst_ref=dst.at[it], send_sem=mid_send.at[1],
                        recv_sem=mid_recv.at[sem], device_id=(sub, cs), device_id_type=MESH,
                    ).wait_recv()
                cross_ref[...] += mid_head[it] * times(mid_tail[it], mid_perm[...])

        moved[0].wait_recv()
        curve = curve - cross_ref[...]
        gp = con_recv[slot].astype(F32)
        for k in range(SLOTS):
            image = jnp.dot(chosen(own, gp, k).astype(BF16), mortar_ref[0, k], preferred_element_type=F32)
            jump = (image - block(g, 2 + k)) * live(own, k)
            curve += jump * jump
        norm = jnp.sum(norm, axis=1, keepdims=True)
        curve = jnp.sum(curve, axis=1, keepdims=True)
        packed = jnp.where(lane == row, norm, 0.0) + jnp.where(lane == row + rows, curve, 0.0)
        total = jnp.sum(packed, axis=0, keepdims=True)
        for r, (f, stride, digit, base) in enumerate(rounds):
            sum_send[it, r] = total
            sum_recv[it, r, digit] = total
            sends = []
            for j in sorted(range(1, f), key=lambda j: abs(2 * j - f)):
                copy = remote(
                    sum_send.at[it, r], sum_recv.at[it, r, digit], sum_ssem.at[it, r, j], sum_rsem.at[it, r, digit],
                    base + lax.rem(digit + j, f) * stride, cs,
                )
                copy.start()
                sends.append(copy)
            for j in range(1, f):
                source = lax.rem(digit + j, f)
                remote(
                    sum_send.at[it, r], sum_recv.at[it, r, source], sum_ssem.at[it, r, j], sum_rsem.at[it, r, source],
                    base + source * stride, cs,
                ).wait_recv()
            total = sum_recv[it, r, 0]
            for d in range(1, f):
                total = total + sum_recv[it, r, d]
            for copy in sends:
                copy.wait_send()
        tot_ref[...] = total

        @pl.when(it == ITERS - 1)
        def _():
            for copy in to_cases():
                copy.start()

        if halfway:
            @pl.when(me == 0)
            def _():
                moved[1].wait_recv()
                mid_first(it).wait_send()

            @pl.when(me == last)
            def _():
                mid_last(it).wait_send()
        moved[2].wait_recv()
        for copy in moved:
            copy.wait_send()
        sg = [times(prev_recv[slot], perm_ref[0]), times(next_recv[slot], perm_ref[1])]
        wide = jnp.broadcast_to(total, (rows, BLK))
        top = jnp.sum(jnp.where(lane == row, wide, 0.0), axis=1, keepdims=True)
        bottom = jnp.sum(jnp.where(lane == row + rows, wide, 0.0), axis=1, keepdims=True)
        step = top / bottom
        step_wide = jnp.broadcast_to(step, (rows, BLK))

        clipped = []
        for b in range(g.shape[1] // BLK):
            at = slice(b * BLK, (b + 1) * BLK)
            fresh = x_ref[:, at] - step_wide * block(g, b)
            if 2 <= b < 2 + SLOTS:
                kept = jnp.maximum(fresh, 0.0)
                clipped.append((kept - fresh).astype(BF16))
                fresh = kept
            x_ref[:, at] = fresh
        for k in range(SLOTS):
            at = slice(k * BLK, (k + 1) * BLK)
            xp_ref[:, at] = jnp.maximum(xp_ref[:, at] - step_wide * block(gp, k), 0.0)
        for side in range(2):
            sx_ref[side] = sx_ref[side] - step_wide * sg[side]

        @pl.when(it < ITERS - 1)
        def _():
            pushed = jnp.dot(
                jnp.concatenate(clipped, axis=1), k_ref[2 * BLK:(2 + SLOTS) * BLK, :], preferred_element_type=F32
            )
            for b in range(g.shape[1] // BLK):
                at = slice(b * BLK, (b + 1) * BLK)
                kx_ref[:, at] = kx_ref[:, at] - step_wide * q_ref[:, at] + block(pushed, b)

        return carry

    lax.fori_loop(0, ITERS, body, 0)

    tot_recv[cs] = tot_ref[...]
    sends = to_cases()
    out_ref[...] = x_ref[...]
    for j in range(1, nc):
        source = lax.rem(cs + j, nc)
        remote(tot_ref, tot_recv.at[source], tot_ssem.at[j], tot_rsem.at[source], me, source).wait_recv()
    for copy in sends:
        copy.wait_send()
    total = tot_recv[0]
    for d in range(1, nc):
        total = total + tot_recv[d]
    flat = lax.broadcasted_iota(jnp.int32, (1, BLK), 1)
    whole = jnp.sum(jnp.where(flat < rows, total, 0.0), axis=1, keepdims=True)
    norm_ref[0] = jnp.sqrt(whole)[0, 0]


def solution(mesh):
    n, nc = mesh.shape["sub"], mesh.shape["case"]
    factors = radices(n)
    chunks = 3

    def on_device(multipliers, right_side, dual_ops, glue_match, mortar, contact_ids, contact_count):
        rows, order = multipliers.shape
        top = max(factors)
        rounds = len(factors)
        vmem = pl.BlockSpec(memory_space=pltpu.VMEM)
        smem = pl.BlockSpec(memory_space=pltpu.SMEM)
        dma = pltpu.SemaphoreType.DMA
        slots = ITERS + 1
        return pl.pallas_call(
            functools.partial(kernel, n, nc, factors, chunks),
            out_shape=(
                jax.ShapeDtypeStruct((rows, order), F32),
                jax.ShapeDtypeStruct((1,), F32),
            ),
            in_specs=[pl.BlockSpec(memory_space=pltpu.HBM)] * 7,
            out_specs=(vmem, smem),
            scratch_shapes=[
                pltpu.VMEM((rows, order), F32),
                pltpu.VMEM((rows, order), F32),
                pltpu.VMEM(glue_match.shape, jnp.int32),
                pltpu.VMEM(mortar.shape, BF16),
                pltpu.SMEM(contact_ids.shape, jnp.int32),
                pltpu.SMEM(contact_count.shape, jnp.int32),
                pltpu.VMEM((order, order), BF16),
                pltpu.VMEM((rows, order), F32),
                pltpu.VMEM((rows, order), F32),
                pltpu.VMEM((rows, order), F32),
                pltpu.VMEM((rows, order), F32),
                pltpu.VMEM((2, rows, BLK), F32),
                pltpu.VMEM((rows, SLOTS * BLK), F32),
                pltpu.VMEM((2, BLK, BLK), BF16),
                pltpu.VMEM((SLOTS * SLOTS + 2 * SLOTS, BLK), F32),
                pltpu.VMEM((SLOTS * SLOTS + 2 * SLOTS, BLK), F32),
                pltpu.VMEM((SLOTS, BLK, BLK), BF16),
                pltpu.VMEM((slots, rows, SLOTS * BLK), BF16),
                pltpu.VMEM((slots, rows, SLOTS * BLK), BF16),
                pltpu.VMEM((slots, rows, BLK), F32),
                pltpu.VMEM((slots, rows, BLK), F32),
                pltpu.VMEM((rows, BLK), F32),
                pltpu.VMEM((BLK, BLK), BF16),
                pltpu.VMEM((ITERS, rows, BLK), F32),
                pltpu.VMEM((ITERS, rows, BLK), F32),
                pltpu.VMEM((ITERS, rounds, 1, BLK), F32),
                pltpu.VMEM((ITERS, rounds, top, 1, BLK), F32),
                pltpu.VMEM((1, BLK), F32),
                pltpu.VMEM((nc, 1, BLK), F32),
                dma((6,)),
                dma((chunks,)),
                dma((slots, 3)),
                dma((slots, 3)),
                dma((2,)),
                dma((2,)),
                dma((max(nc - 1, 1),)),
                dma((max(nc - 1, 1),)),
                dma((ITERS, rounds, top)),
                dma((ITERS, rounds, top)),
                dma((nc,)),
                dma((nc,)),
                dma((3,)),
                dma((1 + 2 * ITERS,)),
            ],
            compiler_params=pltpu.CompilerParams(
                collective_id=0, has_side_effects=True, vmem_limit_bytes=58 * 1024 * 1024
            ),
        )(multipliers, right_side, dual_ops, glue_match, mortar, contact_ids, contact_count)

    in_specs = (
        P("case", "sub"),
        P("case", "sub"),
        P("sub", None),
        P("sub", None, None),
        P("sub", None, None, None),
        P("sub", None),
        P("sub"),
    )
    return jax.shard_map(
        on_device, mesh=mesh, in_specs=in_specs, out_specs=(P("case", "sub"), P()), check_vma=False
    )
```
